128 devices in a mesh: cam: 4 (over y_hi, core), frame: 16 (over x, z), tok: 2 (over y_lo).
Axes of the slice: x: 4, y: 4 (y_hi: 2, y_lo: 2; y = y_hi * 2 + y_lo), z: 4, core: 2. Of those that a mesh axis runs over, the one named last changes fastest.
Arguments:
- latents: bfloat16 [4, 16, 768, 1152], P('cam', 'frame', 'tok'), may hold values from -12 to 12
- actions: int32 [16, 8], P('frame'), may hold values from 0 to 255
- history_start: int32 [4], replicated, may hold values from 0 to 8
- mod_table: bfloat16 [256, 4608], replicated, may hold values from -1 to 1
- w_query: bfloat16 [1152, 1152], replicated, may hold values from -1 to 1
- w_key: bfloat16 [1152, 1152], replicated, may hold values from -1 to 1
- w_value: bfloat16 [1152, 1152], replicated, may hold values from -0.1875 to 0.1875
- w_out: bfloat16 [1152, 1152], replicated, may hold values from -0.1875 to 0.1875
- t_query: bfloat16 [1152, 1152], replicated, may hold values from -1 to 1
- t_key: bfloat16 [1152, 1152], replicated, may hold values from -1 to 1
- t_value: bfloat16 [1152, 1152], replicated, may hold values from -0.1875 to 0.1875
- t_out: bfloat16 [1152, 1152], replicated, may hold values from -0.1875 to 0.1875
Outputs:
- block_out: bfloat16 [4, 16, 768, 1152], P('cam', 'frame', 'tok')
The draws below stay inside these ranges and needn't reach their ends.
All inputs are finite; a program needn't handle non-finite values.
Results may differ from the reference program's by a relative error of at most 0.017.
Values may be sent and summed in bfloat16 or wider, within the bound.
No kernel may reach another device: no remote copies, remote signals or barrier semaphores. Data moves between devices by JAX's collectives and lax.ppermute only.
A program may use at most 192 MiB of HBM per device.

```python
import math
import jax
import jax.numpy as jnp
from jax import lax

D = 1152
HEADS = 16
SPATIAL = 768
CAMS = 4
FRAMES = 16
ACT = 8
VOCAB = 256


def drawn_weight(key):
    base = jax.random.truncated_normal(key, -6.0, 6.0, (D, D), jnp.float32) / math.sqrt(D)
    return base.astype(jnp.bfloat16)


def draw_latents(key, part):
    key = jax.random.fold_in(key, 7)
    key_noise = jax.random.fold_in(key, 0)
    noise = jax.random.truncated_normal(key_noise, -6.0, 6.0, (CAMS, FRAMES, SPATIAL, D), jnp.float32)
    return noise.astype(jnp.bfloat16)


def draw_w_query(key, part):
    key = jax.random.fold_in(key, 11)
    return drawn_weight(key)


def draw_w_key(key, part):
    key = jax.random.fold_in(key, 12)
    return drawn_weight(key)


def draw_t_query(key, part):
    key = jax.random.fold_in(key, 13)
    return drawn_weight(key)


def draw_t_key(key, part):
    key = jax.random.fold_in(key, 14)
    return drawn_weight(key)


def with_ends(values, rng, least, largest):
    longest = values.shape.index(max(values.shape))
    spots = []
    for shift in (0, 1):
        where = [jax.random.randint(jax.random.fold_in(rng, axis), (), 0, length) for axis, length in enumerate(values.shape)]
        where[longest] = (where[longest] + shift) % values.shape[longest]
        spots.append(tuple(where))
    return values.at[spots[0]].set(least).at[spots[1]].set(largest)


def bell_draw(stream_key, shape, scale, most, kind=jnp.bfloat16):
    return jnp.clip(scale * jax.random.normal(stream_key, shape, jnp.float32), -most, most).astype(kind)


def setup_inputs(seed: int = 0) -> dict:
    key_list = jax.random.split(jax.random.key(seed), 13)
    latents = draw_latents(jax.random.fold_in(key_list[12], 71), 0)
    actions = with_ends(jax.random.randint(key_list[1], (FRAMES, ACT), 0, VOCAB), jax.random.fold_in(key_list[1], 1), 0, VOCAB - 1).astype(jnp.int32)
    history_start = with_ends(jax.random.randint(key_list[2], (CAMS,), 0, FRAMES // 2 + 1), jax.random.fold_in(key_list[2], 1), 0, (FRAMES // 2 + 1) - 1).astype(jnp.int32)
    mod_table = bell_draw(key_list[3], (VOCAB, 4 * D), 0.2, 1.0)
    w_query = draw_w_query(jax.random.fold_in(key_list[12], 71), 0)
    w_key = draw_w_key(jax.random.fold_in(key_list[12], 71), 0)
    w_value = bell_draw(key_list[6], (D, D), D ** -0.5, 0.1875)
    w_out = bell_draw(key_list[7], (D, D), D ** -0.5, 0.1875)
    t_query = draw_t_query(jax.random.fold_in(key_list[12], 71), 0)
    t_key = draw_t_key(jax.random.fold_in(key_list[12], 71), 0)
    t_value = bell_draw(key_list[10], (D, D), D ** -0.5, 0.1875)
    t_out = bell_draw(key_list[11], (D, D), D ** -0.5, 0.1875)
    return {"latents": latents, "actions": actions, "history_start": history_start, "mod_table": mod_table, "w_query": w_query, "w_key": w_key, "w_value": w_value, "w_out": w_out, "t_query": t_query, "t_key": t_key, "t_value": t_value, "t_out": t_out}


def normalize(values):
    mean = lax.optimization_barrier(jnp.mean(values, axis=-1, keepdims=True))
    centred = values - mean
    spread = lax.optimization_barrier(jnp.mean(centred * centred, axis=-1, keepdims=True))
    return centred * lax.rsqrt(spread + 1e-06)

def project(values, weight):
    return jnp.dot(values, weight, preferred_element_type=jnp.float32).astype(jnp.bfloat16)

def reference(latents, actions, history_start, mod_table, w_query, w_key, w_value, w_out, t_query, t_key, t_value, t_out):
    head_dim = D // HEADS
    scale = 1.0 / math.sqrt(head_dim)
    counts = lax.optimization_barrier(jnp.sum((actions[:, :, None] == jnp.arange(VOCAB, dtype=jnp.int32)[None, None, :]).astype(jnp.float32), axis=1))
    cond = jnp.dot(counts.astype(jnp.bfloat16), mod_table, preferred_element_type=jnp.float32)
    shift_one = cond[None, :, None, 0:D]
    scale_one = cond[None, :, None, D:2 * D]
    shift_two = cond[None, :, None, 2 * D:3 * D]
    scale_two = cond[None, :, None, 3 * D:4 * D]
    stream = latents.astype(jnp.float32)
    hidden = (normalize(stream) * (1.0 + scale_one) + shift_one).astype(jnp.bfloat16)
    shape = (CAMS, FRAMES, SPATIAL, HEADS, head_dim)
    query = project(hidden, w_query).reshape(shape)
    keys = project(hidden, w_key).reshape(shape)
    values = project(hidden, w_value).reshape(shape)
    keys_all = jnp.concatenate([jnp.roll(keys, 1, axis=0), keys, jnp.roll(keys, -1, axis=0)], axis=2)
    values_all = jnp.concatenate([jnp.roll(values, 1, axis=0), values, jnp.roll(values, -1, axis=0)], axis=2)

    def cross(block):
        qb, kb, vb = block
        scores = jnp.einsum('qhe,khe->hqk', qb.astype(jnp.float32), kb.astype(jnp.float32)) * scale
        weights = jax.nn.softmax(scores, axis=-1).astype(jnp.bfloat16)
        mixed = jnp.einsum('hqk,khe->qhe', weights.astype(jnp.float32), vb.astype(jnp.float32))
        return mixed.astype(jnp.bfloat16)
    flat = (CAMS * FRAMES, 3 * SPATIAL, HEADS, head_dim)
    attended = lax.map(cross, (query.reshape(CAMS * FRAMES, SPATIAL, HEADS, head_dim), keys_all.reshape(flat), values_all.reshape(flat)))
    attended = attended.reshape(CAMS, FRAMES, SPATIAL, D)
    first = (stream + jnp.dot(attended, w_out, preferred_element_type=jnp.float32)).astype(jnp.bfloat16)
    first_f = first.astype(jnp.float32)
    hidden_two = (normalize(first_f) * (1.0 + scale_two) + shift_two).astype(jnp.bfloat16)
    query_two = project(hidden_two, t_query).reshape(shape)
    keys_two = project(hidden_two, t_key).reshape(shape)
    values_two = project(hidden_two, t_value).reshape(shape)
    later = jnp.arange(FRAMES, dtype=jnp.int32)[:, None]
    earlier = jnp.arange(FRAMES, dtype=jnp.int32)[None, :]

    def temporal(block):
        qc, kc, vc, start = block
        allowed = (earlier <= later) & ((earlier >= start) | (earlier == later))
        scores = jnp.einsum('fthe,gthe->fgth', qc.astype(jnp.float32), kc.astype(jnp.float32)) * scale
        scores = jnp.where(allowed[:, :, None, None], scores, -1e+30)
        weights = jax.nn.softmax(scores, axis=1)
        mixed = jnp.einsum('fgth,gthe->fthe', weights, vc.astype(jnp.float32))
        return mixed.astype(jnp.bfloat16)
    mixed_two = lax.map(temporal, (query_two, keys_two, values_two, history_start))
    mixed_two = mixed_two.reshape(CAMS, FRAMES, SPATIAL, D)
    return (first_f + jnp.dot(mixed_two, t_out, preferred_element_type=jnp.float32)).astype(jnp.bfloat16)
```

```python
import functools
import math

import jax
import jax.numpy as jnp
from jax import lax
from jax.experimental import pallas as pl
from jax.experimental.pallas import tpu as pltpu
from jax.sharding import PartitionSpec as P

HEADS = 16
VMEM_LIMIT = 48 * 1024 * 1024
F32, BF16 = jnp.float32, jnp.bfloat16
NT = (((1,), (1,)), ((), ()))
TN = (((0,), (0,)), ((), ()))
RING = ("cam", "tok")


def modulated(values, shift, scale):
    mean = jnp.mean(values, axis=-1, keepdims=True)
    centred = values - mean
    spread = jnp.mean(centred * centred, axis=-1, keepdims=True)
    return (centred * lax.rsqrt(spread + 1e-06) * (1.0 + scale) + shift).astype(BF16)


def stacked_queries(query, pair, head_dim):
    start = 2 * pair * head_dim // 128 * 128
    window = query[:, start : start + 256]
    lane = lax.broadcasted_iota(jnp.int32, window.shape, 1) + start
    low = 2 * pair * head_dim
    zero = jnp.zeros((), query.dtype)
    parts = [
        jnp.where((lane >= low + i * head_dim) & (lane < low + (i + 1) * head_dim), window, zero)
        for i in range(2)
    ]
    return jnp.concatenate(parts, axis=0), start


def attend(q_ref, k_ref, vt_ref, old, new, heads):
    count, width = q_ref.shape
    head_dim = width // heads
    top_new, total_new, acc_new = new

    def scores_of(pair):
        stacked, start = stacked_queries(q_ref[...], pair, head_dim)
        scores = lax.dot_general(
            k_ref[:, start : start + 256], stacked, NT, preferred_element_type=F32
        )
        return scores[:, :count], scores[:, count:]

    ahead = scores_of(0)
    for pair in range(heads // 2):
        current = ahead
        if pair + 1 < heads // 2:
            ahead = scores_of(pair + 1)
        for i in range(2):
            head = 2 * pair + i
            scores = current[i]
            rows = slice(head * head_dim, (head + 1) * head_dim)
            from_row = head * head_dim // 16 * 16
            skip = head * head_dim - from_row
            top = jnp.max(scores, axis=0, keepdims=True)
            if old is not None:
                top_old = old[0][head : head + 1, :]
                top = jnp.maximum(top, top_old)
                keep = jnp.exp2(top_old - top)
            weights = jnp.exp2(scores - top)
            total = jnp.sum(weights, axis=0, keepdims=True)
            mixed = jnp.dot(
                vt_ref[from_row : from_row + 80, :],
                weights.astype(BF16),
                preferred_element_type=F32,
            )[skip : skip + head_dim]
            if old is not None:
                total = total + old[1][head : head + 1, :] * keep
                mixed = mixed + old[2][rows, :] * keep
            top_new[head : head + 1, :] = top
            total_new[head : head + 1, :] = total
            acc_new[rows, :] = mixed


def keys_values(hidden, wk_ref, wvt_ref, k_ref, vt_ref):
    k_ref[...] = jnp.dot(hidden[...], wk_ref[...], preferred_element_type=F32).astype(BF16)
    vt_ref[...] = lax.dot_general(
        wvt_ref[...], hidden[...], NT, preferred_element_type=F32
    ).astype(BF16)


def norm_blocks(blocks, cond, column, hidden):
    width = hidden.shape[1]
    shift = cond[0:1, column : column + width]
    scale = cond[0:1, column + width : column + 2 * width]
    at = 0
    for block in blocks:
        rows = block.shape[0]
        hidden[at : at + rows, :] = modulated(block[...].astype(F32), shift, scale)
        at += rows


def first_kernel(
    heads,
    actions,
    table,
    own,
    mate,
    wq,
    wk,
    wvt,
    cond,
    query,
    top,
    total,
    acc,
    hidden,
    k_ref,
    vt_ref,
):
    vocab = table.shape[0]
    width = own.shape[1]
    ids = lax.broadcasted_iota(jnp.int32, (8, vocab), 1)
    counts = jnp.zeros((8, vocab), F32)
    for i in range(actions.shape[1]):
        counts = counts + (ids == actions[0, i]).astype(F32)
    cond[...] = jnp.dot(counts.astype(BF16), table[...], preferred_element_type=F32)
    norm_blocks((own, mate), cond, 0, hidden)
    scale = math.log2(math.e) / math.sqrt(width // heads)
    count = own.shape[0]
    query[...] = (
        jnp.dot(hidden[0:count, :], wq[...], preferred_element_type=F32) * scale
    ).astype(BF16)
    keys_values(hidden, wk, wvt, k_ref, vt_ref)
    attend(query, k_ref, vt_ref, None, (top, total, acc), heads)


def more_kernel(heads, blocks, *refs):
    xs, refs = refs[:blocks], refs[blocks:]
    cond, query, wk, wvt, top, total, acc, top_new, total_new, acc_new, hidden, k_ref, vt_ref = refs
    norm_blocks(xs, cond, 0, hidden)
    keys_values(hidden, wk, wvt, k_ref, vt_ref)
    attend(query, k_ref, vt_ref, (top, total, acc), (top_new, total_new, acc_new), heads)


def last_kernel(heads, blocks, *refs):
    xs, refs = refs[:blocks], refs[blocks:]
    cond, query, wk, wvt, top, total, acc, own, w_out = refs[:9]
    first, hidden_two, top_new, total_new, acc_new, hidden, k_ref, vt_ref = refs[9:]
    width = own.shape[1]
    head_dim = width // heads
    norm_blocks(xs, cond, 0, hidden)
    keys_values(hidden, wk, wvt, k_ref, vt_ref)
    attend(query, k_ref, vt_ref, (top, total, acc), (top_new, total_new, acc_new), heads)
    pieces = [
        acc_new[h * head_dim : (h + 1) * head_dim, :] / total_new[h : h + 1, :]
        for h in range(heads)
    ]
    attended = jnp.concatenate(pieces, axis=0).T.astype(BF16)
    y = own[...].astype(F32) + jnp.dot(attended, w_out[...], preferred_element_type=F32)
    first[...] = y.astype(BF16)
    shift = cond[0:1, 2 * width : 3 * width]
    scale = cond[0:1, 3 * width : 4 * width]
    hidden_two[...] = modulated(first[...].astype(F32), shift, scale)


def temporal_kernel(heads, start_ref, x_ref, wq, wk, wvt, out, hidden, q_ref, k_ref, vt_ref, ot):
    frames, tokens, width = x_ref.shape
    head_dim = width // heads
    groups = tokens // 8
    span = 8 * frames
    x = x_ref[...].astype(F32)
    for g in range(groups):
        hidden[g * span : (g + 1) * span, :] = (
            x[:, 8 * g : 8 * g + 8, :].reshape(span, width).astype(BF16)
        )
    scale = math.log2(math.e) / math.sqrt(head_dim)
    q_ref[...] = (jnp.dot(hidden[...], wq[...], preferred_element_type=F32) * scale).astype(BF16)
    keys_values(hidden, wk, wvt, k_ref, vt_ref)
    key = lax.broadcasted_iota(jnp.int32, (span, span), 0)
    ask = lax.broadcasted_iota(jnp.int32, (span, span), 1)
    same = (key % 8) == (ask % 8)
    frame_k, frame_q = key // 8, ask // 8
    allowed = same & (
        (frame_k == frame_q) | ((frame_k < frame_q) & (frame_k >= start_ref[0]))
    )
    for g in range(groups):
        rows = slice(g * span, (g + 1) * span)
        query = q_ref[rows, :]
        for pair in range(heads // 2):
            stacked, start = stacked_queries(query, pair, head_dim)
            both = lax.dot_general(
                k_ref[rows, start : start + 256], stacked, NT, preferred_element_type=F32
            )
            for i in range(2):
                head = 2 * pair + i
                scores = jnp.where(allowed, both[:, i * span : (i + 1) * span], -1e30)
                top = jnp.max(scores, axis=0, keepdims=True)
                weights = jnp.exp2(scores - top)
                total = jnp.sum(weights, axis=0, keepdims=True)
                from_row = head * head_dim // 16 * 16
                skip = head * head_dim - from_row
                mixed = jnp.dot(
                    vt_ref[from_row : from_row + 80, rows],
                    weights.astype(BF16),
                    preferred_element_type=F32,
                )[skip : skip + head_dim]
                ot[head * head_dim : (head + 1) * head_dim, rows] = mixed / total
    mixed = ot[...].T
    pieces = [mixed[g * span : (g + 1) * span, :].reshape(frames, 8, width) for g in range(groups)]
    out[...] = jnp.concatenate(pieces, axis=1).astype(BF16)


def kernel_call(body, name, outs, scratch, operands, smem=(), flops=0, exps=0):
    vmem = pl.BlockSpec(memory_space=pltpu.VMEM)
    scalar = pl.BlockSpec(memory_space=pltpu.SMEM)
    moved = sum(math.prod(a.shape) * a.dtype.itemsize for a in (*operands, *outs))
    return pl.pallas_call(
        body,
        name=name,
        out_shape=outs,
        in_specs=[scalar if i in smem else vmem for i in range(len(operands))],
        out_specs=jax.tree.map(lambda _: vmem, outs),
        scratch_shapes=scratch,
        compiler_params=pltpu.CompilerParams(vmem_limit_bytes=VMEM_LIMIT),
        cost_estimate=pl.CostEstimate(flops=flops, bytes_accessed=moved, transcendentals=exps),
    )(*operands)


def ring_routes():
    def index(y, core):
        return ((y // 2) * 2 + core) * 2 + y % 2

    places = [(y, core) for y in range(4) for core in range(2)]
    mate = [(index(y, core), index(y, 1 - core)) for y, core in places]
    partner = [(index(y, core), index(y ^ 1, core)) for y, core in places]
    other = [(index(y, core), index(3 - y, 1 - core)) for y, core in places]
    return mate, partner, other


def shards(
    latents,
    actions,
    history_start,
    mod_table,
    w_query,
    w_key,
    w_value,
    w_out,
    t_query,
    t_key,
    t_value,
    t_out,
):
    rows, width = latents.shape[2:]
    heads = HEADS
    frames = lax.axis_size("frame")
    own = latents[0, 0]
    mate, partner, other = ring_routes()
    half, cut = rows // 2, rows // 3
    send = lambda block, route: lax.ppermute(block, RING, route)
    from_mate = send(own, mate)
    other_a = send(own[: 2 * cut], other)
    partner_a = send(own[cut:], partner)
    other_b = send(own[2 * cut :], other)
    partner_b = send(own[:cut], partner)
    mate_a = send(partner_a, mate)
    far_a = send(other_a[:half], partner)
    far_b = send(partner_a[half - cut :], other)
    mate_b = send(partner_b, mate)
    wvt = w_value.T
    tvt = t_value.T

    def sds(shape, dtype):
        return jax.ShapeDtypeStruct(shape, dtype)

    state = [sds((heads, rows), F32), sds((heads, rows), F32), sds((width, rows), F32)]
    unit = 2 * rows * width * width

    def scratch(keys):
        return [
            pltpu.VMEM((keys, width), BF16),
            pltpu.VMEM((keys, width), BF16),
            pltpu.VMEM((width, keys), BF16),
        ]

    def cost(keys):
        return 2 * unit * keys // rows + 4 * rows * keys * 256 * heads

    cond, query, *held = kernel_call(
        functools.partial(first_kernel, heads),
        "cross_first",
        [sds((8, mod_table.shape[1]), F32), sds((rows, width), BF16), *state],
        scratch(2 * rows),
        (actions, mod_table, own, from_mate, w_query, w_key, wvt),
        smem=(0,),
        flops=unit + cost(2 * rows),
    )
    for name, blocks in (
        ("cross_second", (other_a, partner_a, mate_a)),
        ("cross_third", (other_b, partner_b, mate_b)),
    ):
        keys = sum(b.shape[0] for b in blocks)
        held = kernel_call(
            functools.partial(more_kernel, heads, len(blocks)),
            name,
            state,
            scratch(keys),
            (*blocks, cond, query, w_key, wvt, *held),
            flops=cost(keys),
        )
    blocks = (far_a, far_b)
    keys = sum(b.shape[0] for b in blocks)
    first, hidden_two = kernel_call(
        functools.partial(last_kernel, heads, len(blocks)),
        "cross_last",
        [sds((rows, width), BF16), sds((rows, width), BF16)],
        [pltpu.VMEM(s.shape, s.dtype) for s in state] + scratch(keys),
        (*blocks, cond, query, w_key, wvt, *held, own, w_out),
        flops=cost(keys) + unit,
    )
    share = rows // frames
    turned = lax.all_to_all(
        hidden_two.reshape(frames, share, width), "frame", 0, 0, tiled=True
    )
    cam_start = lax.dynamic_slice_in_dim(history_start, lax.axis_index("cam"), 1, 0)
    (mixed,) = kernel_call(
        functools.partial(temporal_kernel, heads),
        "temporal",
        [sds((frames, share, width), BF16)],
        [pltpu.VMEM((rows, width), BF16)] * 3
        + [pltpu.VMEM((width, rows), BF16), pltpu.VMEM((width, rows), F32)],
        (cam_start, turned, t_query, t_key, tvt),
        smem=(0,),
        flops=4 * unit,
    )
    back = lax.all_to_all(mixed, "frame", 0, 0, tiled=True).reshape(rows, width)
    result = first.astype(F32) + jnp.dot(back, t_out, preferred_element_type=F32)
    return result.astype(BF16)[None, None]


def solution(mesh):
    in_specs = (
        P("cam", "frame", "tok", None),
        P("frame", None),
        P(),
        P(),
        P(),
        P(),
        P(),
        P(),
        P(),
        P(),
        P(),
        P(),
    )
    out_specs = P("cam", "frame", "tok", None)
    return jax.shard_map(shards, mesh=mesh, in_specs=in_specs, out_specs=out_specs, check_vma=False)
```

```python
import functools
import math

import jax
import jax.numpy as jnp
from jax import lax
from jax.experimental import pallas as pl
from jax.experimental.pallas import tpu as pltpu
from jax.sharding import PartitionSpec as P

HEADS = 16
VMEM_LIMIT = 26 * 1024 * 1024
F32, BF16 = jnp.float32, jnp.bfloat16
NT = (((1,), (1,)), ((), ()))
TN = (((0,), (0,)), ((), ()))
RING = ("cam", "tok")


def modulated(values, shift, scale):
    mean = jnp.mean(values, axis=-1, keepdims=True)
    centred = values - mean
    spread = jnp.mean(centred * centred, axis=-1, keepdims=True)
    return (centred * lax.rsqrt(spread + 1e-06) * (1.0 + scale) + shift).astype(BF16)


def stacked_queries(query, pair, head_dim):
    start = 2 * pair * head_dim // 128 * 128
    window = query[:, start : start + 256]
    lane = lax.broadcasted_iota(jnp.int32, window.shape, 1) + start
    low = 2 * pair * head_dim
    zero = jnp.zeros((), query.dtype)
    parts = [
        jnp.where((lane >= low + i * head_dim) & (lane < low + (i + 1) * head_dim), window, zero)
        for i in range(2)
    ]
    return jnp.concatenate(parts, axis=0), start


def head_rows(head, head_dim):
    low = head * head_dim
    start = low // 16 * 16
    return slice(low, low + head_dim), slice(start, start + 80), slice(low - start, low - start + head_dim)


def attend(q_ref, k_ref, vt_ref, old, new, heads):
    count, width = q_ref.shape
    head_dim = width // heads
    top_new, total_new, acc_new = new

    def scores_of(pair, keys):
        stacked, start = stacked_queries(q_ref[...], pair, head_dim)
        scores = lax.dot_general(
            k_ref[0:keys, start : start + 256], stacked, NT, preferred_element_type=F32
        )
        return scores[:, :count], scores[:, count:]

    if old is None:
        for pair in range(heads // 2):
            for i, scores in enumerate(scores_of(pair, 64)):
                head = 2 * pair + i
                top_new[head : head + 1, :] = jnp.max(scores, axis=0, keepdims=True)
    else:
        top_new[...] = old[0][...]
    ahead = scores_of(0, k_ref.shape[0])
    for pair in range(heads // 2):
        current = ahead
        if pair + 1 < heads // 2:
            ahead = scores_of(pair + 1, k_ref.shape[0])
        for i in range(2):
            head = 2 * pair + i
            scores = current[i]
            rows, window, inside = head_rows(head, head_dim)
            top = top_new[head : head + 1, :]
            weights = jnp.exp2(scores - top)
            total = jnp.sum(weights, axis=0, keepdims=True)
            mixed = jnp.dot(
                vt_ref[window, :], weights.astype(BF16), preferred_element_type=F32
            )[inside]
            if old is not None:
                total = total + old[1][head : head + 1, :]
                mixed = mixed + old[2][rows, :]
            total_new[head : head + 1, :] = total
            acc_new[rows, :] = mixed

    safe = jnp.max(total_new[...]) < 2.0**60

    @pl.when(jnp.logical_not(safe))
    def _():
        attend_with_maximum(q_ref, k_ref, vt_ref, old, new, heads)


def attend_with_maximum(q_ref, k_ref, vt_ref, old, new, heads):
    count, width = q_ref.shape
    head_dim = width // heads
    top_new, total_new, acc_new = new

    @pl.loop(0, count // 128 * heads)
    def _(step):
        head = step % heads
        at = pl.ds(pl.multiple_of(step // heads * 128, 128), 128)
        low = head * head_dim
        start = low // 128 * 128
        columns = pl.ds(pl.multiple_of(jnp.minimum(start, width - 256), 128), 256)
        skip = low - jnp.minimum(start, width - 256)
        from_row = low // 16 * 16
        window = pl.ds(pl.multiple_of(from_row, 16), 80)
        rows = pl.ds(pl.multiple_of(low, 8), head_dim)
        mine = lax.broadcasted_iota(jnp.int32, (heads, 128), 0) == head
        query = q_ref[at, columns]
        lane = lax.broadcasted_iota(jnp.int32, query.shape, 1)
        query = jnp.where((lane >= skip) & (lane < skip + head_dim), query, jnp.zeros((), BF16))
        scores = lax.dot_general(k_ref[:, columns], query, NT, preferred_element_type=F32)
        top = jnp.max(scores, axis=0, keepdims=True)
        if old is not None:
            top_old = jnp.sum(jnp.where(mine, old[0][:, at], 0.0), axis=0, keepdims=True)
            top = jnp.maximum(top, top_old)
            keep = jnp.exp2(top_old - top)
        weights = jnp.exp2(scores - top)
        total = jnp.sum(weights, axis=0, keepdims=True)
        mixed = jnp.dot(vt_ref[window, :], weights.astype(BF16), preferred_element_type=F32)
        mixed = jnp.where(low == from_row, mixed[:head_dim], mixed[80 - head_dim :])
        if old is not None:
            total_old = jnp.sum(jnp.where(mine, old[1][:, at], 0.0), axis=0, keepdims=True)
            total = total + total_old * keep
            mixed = mixed + old[2][rows, at] * keep
        top_new[:, at] = jnp.where(mine, top, top_new[:, at])
        total_new[:, at] = jnp.where(mine, total, total_new[:, at])
        acc_new[rows, at] = mixed


def keys_values(hidden, wk_ref, wvt_ref, k_ref, vt_ref):
    k_ref[...] = jnp.dot(hidden[...], wk_ref[...], preferred_element_type=F32).astype(BF16)
    vt_ref[...] = lax.dot_general(
        wvt_ref[...], hidden[...], NT, preferred_element_type=F32
    ).astype(BF16)


def norm_blocks(blocks, cond, column, hidden):
    width = hidden.shape[1]
    shift = cond[0:1, column : column + width]
    scale = cond[0:1, column + width : column + 2 * width]
    at = 0
    for block in blocks:
        rows = block.shape[0]
        hidden[at : at + rows, :] = modulated(block[...].astype(F32), shift, scale)
        at += rows


def condition(actions, table):
    vocab = table.shape[0]
    ids = lax.broadcasted_iota(jnp.int32, (8, vocab), 1)
    counts = jnp.zeros((8, vocab), F32)
    for i in range(actions.shape[1]):
        counts = counts + (ids == actions[0, i]).astype(F32)
    return jnp.dot(counts.astype(BF16), table, preferred_element_type=F32)


def fetch(pairs, sems):
    copies = [pltpu.make_async_copy(src, dst, sems.at[i]) for i, (src, dst) in enumerate(pairs)]
    for copy in copies:
        copy.start()
    return copies


def first_kernel(heads, *refs):
    actions, table, own, mate, wq, wk, wv = refs[:7]
    cond, query, wk_v, wvt, top, total, acc = refs[7:14]
    table_v, own_v, wq_v, wv_v, hidden, k_ref, vt_ref, sems = refs[14:]
    count, width = own_v.shape
    pairs = ((table, table_v), (own, own_v), (wq, wq_v), (wk, wk_v), (wv, wv_v))
    into = fetch(pairs, sems)
    into[0].wait()
    cond[...] = condition(actions, table_v[...])
    into[1].wait()
    norm_blocks((own_v, mate), cond, 0, hidden)
    into[2].wait()
    scale = math.log2(math.e) / math.sqrt(width // heads)
    query[...] = (
        jnp.dot(hidden[0:count, :], wq_v[...], preferred_element_type=F32) * scale
    ).astype(BF16)
    into[3].wait()
    into[4].wait()
    wvt[...] = wv_v[...].T
    keys_values(hidden, wk_v, wvt, k_ref, vt_ref)
    attend(query, k_ref, vt_ref, None, (top, total, acc), heads)


def more_kernel(heads, blocks, *refs):
    xs, refs = refs[:blocks], refs[blocks:]
    cond, query, wk, wvt, top, total, acc, top_new, total_new, acc_new = refs[:10]
    hidden, k_ref, vt_ref = refs[10:]
    norm_blocks(xs, cond, 0, hidden)
    keys_values(hidden, wk, wvt, k_ref, vt_ref)
    attend(query, k_ref, vt_ref, (top, total, acc), (top_new, total_new, acc_new), heads)


def last_kernel(heads, blocks, *refs):
    xs, refs = refs[:blocks], refs[blocks:]
    cond, query, wk, wvt, top, total, acc, own, w_out, first, hidden_two = refs[:11]
    top_new, total_new, acc_new, hidden, k_ref, vt_ref = refs[11:]
    width = own.shape[1]
    head_dim = width // heads
    norm_blocks(xs, cond, 0, hidden)
    keys_values(hidden, wk, wvt, k_ref, vt_ref)
    attend(query, k_ref, vt_ref, (top, total, acc), (top_new, total_new, acc_new), heads)
    pieces = [
        acc_new[h * head_dim : (h + 1) * head_dim, :] * (1.0 / total_new[h : h + 1, :])
        for h in range(heads)
    ]
    attended = jnp.concatenate(pieces, axis=0).T.astype(BF16)
    y = own[...].astype(F32) + jnp.dot(attended, w_out[...], preferred_element_type=F32)
    rounded = y.astype(BF16)
    first[...] = rounded
    hidden_two[...] = modulated(
        rounded.astype(F32),
        cond[0:1, 2 * width : 3 * width],
        cond[0:1, 3 * width : 4 * width],
    )


def temporal_kernel(heads, *refs):
    history_start, x_ref, wq, wk, wv, out = refs[:6]
    hidden, q_ref, k_ref, vt_ref, ot = refs[6:]
    frames, tokens, width = x_ref.shape
    head_dim = width // heads
    groups = tokens // 8
    span = 8 * frames
    x = x_ref[...].astype(F32)
    for g in range(groups):
        hidden[g * span : (g + 1) * span, :] = (
            x[:, 8 * g : 8 * g + 8, :].reshape(span, width).astype(BF16)
        )
    vt_ref[...] = jnp.dot(hidden[...], wv[...], preferred_element_type=F32).T.astype(BF16)
    scale = math.log2(math.e) / math.sqrt(head_dim)
    q_ref[...] = (jnp.dot(hidden[...], wq[...], preferred_element_type=F32) * scale).astype(BF16)
    k_ref[...] = jnp.dot(hidden[...], wk[...], preferred_element_type=F32).astype(BF16)
    cam_start = history_start[lax.axis_index("cam")]
    key = lax.broadcasted_iota(jnp.int32, (span, span), 0)
    ask = lax.broadcasted_iota(jnp.int32, (span, span), 1)
    same = (key % 8) == (ask % 8)
    frame_k, frame_q = key // 8, ask // 8
    allowed = same & ((frame_k == frame_q) | ((frame_k < frame_q) & (frame_k >= cam_start)))
    spans = [slice(g * span, (g + 1) * span) for g in range(groups)]

    def scores_of(pair):
        out = []
        for rows in spans:
            stacked, start = stacked_queries(q_ref[rows, :], pair, head_dim)
            both = lax.dot_general(
                k_ref[rows, start : start + 256], stacked, NT, preferred_element_type=F32
            )
            out.append((both[:, :span], both[:, span:]))
        return out

    ahead = scores_of(0)
    for pair in range(heads // 2):
        current = ahead
        if pair + 1 < heads // 2:
            ahead = scores_of(pair + 1)
        work = [
            (2 * pair + i, g, jnp.where(allowed, current[g][i], -1e30))
            for i in range(2)
            for g in range(groups)
        ]
        tops = [jnp.max(scores, axis=0, keepdims=True) for _, _, scores in work]
        weights = [jnp.exp2(item[2] - top) for item, top in zip(work, tops)]
        totals = [jnp.sum(w, axis=0, keepdims=True) for w in weights]
        for (head, g, _), w, total in zip(work, weights, totals):
            rows, window, inside = head_rows(head, head_dim)
            mixed = jnp.dot(
                vt_ref[window, spans[g]], w.astype(BF16), preferred_element_type=F32
            )[inside]
            ot[rows, spans[g]] = mixed * (1.0 / total)
    mixed = ot[...].T
    pieces = [mixed[g * span : (g + 1) * span, :].reshape(frames, 8, width) for g in range(groups)]
    out[...] = jnp.concatenate(pieces, axis=1).astype(BF16)


def output_kernel(first, mixed, t_out, out):
    rows, width = mixed.shape
    y = first[...].astype(F32) + jnp.dot(mixed[...], t_out[...], preferred_element_type=F32)
    out[...] = y.astype(BF16).reshape(out.shape)


def kernel_call(body, name, outs, scratch, operands, kinds, flops=0):
    space = {"s": pltpu.SMEM, "v": pltpu.VMEM, "h": pltpu.HBM}
    operands = [
        pltpu.with_memory_space_constraint(a, pltpu.HBM) if kind == "h" else a
        for a, kind in zip(operands, kinds)
    ]
    moved = sum(math.prod(a.shape) * a.dtype.itemsize for a in (*operands, *outs))
    return pl.pallas_call(
        body,
        name=name,
        out_shape=outs,
        in_specs=[pl.BlockSpec(memory_space=space[kind]) for kind in kinds],
        out_specs=[pl.BlockSpec(memory_space=pltpu.VMEM) for _ in outs],
        scratch_shapes=scratch,
        compiler_params=pltpu.CompilerParams(vmem_limit_bytes=VMEM_LIMIT),
        cost_estimate=pl.CostEstimate(flops=flops, bytes_accessed=moved, transcendentals=0),
    )(*operands)


def ring_routes():
    def index(y, core):
        return ((y // 2) * 2 + core) * 2 + y % 2

    places = [(y, core) for y in range(4) for core in range(2)]
    mate = [(index(y, core), index(y, 1 - core)) for y, core in places]
    partner = [(index(y, core), index(y ^ 1, core)) for y, core in places]
    other = [(index(y, core), index(3 - y, 1 - core)) for y, core in places]
    return mate, partner, other


def shards(
    latents,
    actions,
    history_start,
    mod_table,
    w_query,
    w_key,
    w_value,
    w_out,
    t_query,
    t_key,
    t_value,
    t_out,
):
    rows, width = latents.shape[2:]
    heads = HEADS
    frames = lax.axis_size("frame")
    own = latents[0, 0]
    mate, partner, other = ring_routes()
    half = rows // 2

    def sds(shape, dtype):
        return jax.ShapeDtypeStruct(shape, dtype)

    def buffer(*shape, dtype=BF16):
        return pltpu.VMEM(shape, dtype)

    def send(block, route):
        return lax.ppermute(block, RING, route)

    def projected(keys):
        return [buffer(keys, width), buffer(keys, width), buffer(width, keys)]

    def cost(keys):
        return 2 * unit * keys // rows + 4 * rows * keys * 256 * heads

    unit = 2 * rows * width * width
    weight = buffer(width, width)
    state = [sds((heads, rows), F32), sds((heads, rows), F32), sds((width, rows), F32)]
    from_other = send(own, other)
    from_partner = send(own, partner)
    from_mate = send(own, mate)
    cond, query, wk, wvt, *held = kernel_call(
        functools.partial(first_kernel, heads),
        "cross_first",
        [sds((8, 4 * width), F32), sds((rows, width), BF16)]
        + [sds((width, width), BF16)] * 2
        + state,
        [buffer(*mod_table.shape), buffer(rows, width), weight, weight]
        + projected(2 * rows)
        + [pltpu.SemaphoreType.DMA((5,))],
        (actions, mod_table, own, from_mate, w_query, w_key, w_value),
        "shhvhhh",
        flops=unit + cost(2 * rows),
    )
    from_other, from_partner, held = lax.optimization_barrier((from_other, from_partner, held))
    far_a = send(from_other[:half], partner)
    far_b = send(from_partner[half:], other)
    mate_partner = send(from_partner, mate)
    held = kernel_call(
        functools.partial(more_kernel, heads, 2),
        "cross_second",
        state,
        projected(2 * rows),
        (from_other, from_partner, cond, query, wk, wvt, *held),
        "v" * 9,
        flops=cost(2 * rows),
    )
    first, hidden_two = kernel_call(
        functools.partial(last_kernel, heads, 3),
        "cross_last",
        [sds((rows, width), BF16), sds((rows, width), BF16)],
        [pltpu.VMEM(s.shape, s.dtype) for s in state] + projected(2 * rows),
        (mate_partner, far_a, far_b, cond, query, wk, wvt, *held, own, w_out),
        "v" * 12,
        flops=cost(2 * rows) + unit,
    )
    share = rows // frames
    turned = lax.all_to_all(
        hidden_two.reshape(frames, share, width), "frame", 0, 0, tiled=True
    )
    (mixed,) = kernel_call(
        functools.partial(temporal_kernel, heads),
        "temporal",
        [sds((frames, share, width), BF16)],
        [buffer(rows, width)] * 3 + [buffer(width, rows), buffer(width, rows, dtype=F32)],
        (history_start, turned, t_query, t_key, t_value),
        "svvvv",
        flops=4 * unit,
    )
    back = lax.all_to_all(mixed, "frame", 0, 0, tiled=True).reshape(rows, width)
    (result,) = kernel_call(
        output_kernel,
        "output",
        [sds((1, 1, rows, width), BF16)],
        [],
        (first, back, t_out),
        "vvv",
        flops=unit,
    )
    return result


def solution(mesh):
    in_specs = (
        P("cam", "frame", "tok", None),
        P("frame", None),
        P(),
        P(),
        P(),
        P(),
        P(),
        P(),
        P(),
        P(),
        P(),
        P(),
    )
    out_specs = P("cam", "frame", "tok", None)
    return jax.shard_map(shards, mesh=mesh, in_specs=in_specs, out_specs=out_specs, check_vma=False)
```

```python
import functools
import math

import jax
import jax.numpy as jnp
from jax import lax
from jax.experimental import pallas as pl
from jax.experimental.pallas import tpu as pltpu
from jax.sharding import PartitionSpec as P

HEADS = 16
VMEM_LIMIT = 26 * 1024 * 1024
F32, BF16 = jnp.float32, jnp.bfloat16
NT = (((1,), (1,)), ((), ()))
TN = (((0,), (0,)), ((), ()))
RING = ("cam", "tok")


def modulated(values, shift, scale):
    mean = jnp.mean(values, axis=-1, keepdims=True)
    centred = values - mean
    spread = jnp.mean(centred * centred, axis=-1, keepdims=True)
    return (centred * lax.rsqrt(spread + 1e-06) * (1.0 + scale) + shift).astype(BF16)


def stacked_queries(query, pair, head_dim):
    start = 2 * pair * head_dim // 128 * 128
    window = query[:, start : start + 256]
    lane = lax.broadcasted_iota(jnp.int32, window.shape, 1) + start
    low = 2 * pair * head_dim
    zero = jnp.zeros((), query.dtype)
    parts = [
        jnp.where((lane >= low + i * head_dim) & (lane < low + (i + 1) * head_dim), window, zero)
        for i in range(2)
    ]
    return jnp.concatenate(parts, axis=0), start


def head_rows(head, head_dim):
    low = head * head_dim
    start = low // 16 * 16
    return slice(low, low + head_dim), slice(start, start + 80), slice(low - start, low - start + head_dim)


def attend(q_ref, k_ref, vt_ref, old, new, heads):
    count, width = q_ref.shape
    head_dim = width // heads
    top_new, total_new, acc_new = new

    def scores_of(pair):
        stacked, start = stacked_queries(q_ref[...], pair, head_dim)
        scores = lax.dot_general(
            k_ref[:, start : start + 256], stacked, NT, preferred_element_type=F32
        )
        return scores[:, :count], scores[:, count:]

    if old is None:
        own_key = q_ref[...] * k_ref[0:count, :]
        owner = lax.broadcasted_iota(jnp.int32, (heads, width), 1) // head_dim
        pick = (owner == lax.broadcasted_iota(jnp.int32, (heads, width), 0)).astype(BF16)
        top_new[...] = lax.dot_general(pick, own_key, NT, preferred_element_type=F32)
    else:
        top_new[...] = old[0][...]
    ahead = scores_of(0)
    for pair in range(heads // 2):
        current = ahead
        if pair + 1 < heads // 2:
            ahead = scores_of(pair + 1)
        for i in range(2):
            head = 2 * pair + i
            scores = current[i]
            rows, window, inside = head_rows(head, head_dim)
            top = top_new[head : head + 1, :]
            weights = jnp.exp2(scores - top)
            total = jnp.sum(weights, axis=0, keepdims=True)
            mixed = jnp.dot(
                vt_ref[window, :], weights.astype(BF16), preferred_element_type=F32
            )[inside]
            if old is not None:
                total = total + old[1][head : head + 1, :]
                mixed = mixed + old[2][rows, :]
            total_new[head : head + 1, :] = total
            acc_new[rows, :] = mixed

    sums = total_new[...]
    safe = (jnp.max(sums) < 2.0**60) & (jnp.min(sums) > 2.0**-60)

    @pl.when(jnp.logical_not(safe))
    def _():
        attend_with_maximum(q_ref, k_ref, vt_ref, old, new, heads)


def attend_with_maximum(q_ref, k_ref, vt_ref, old, new, heads):
    count, width = q_ref.shape
    head_dim = width // heads
    top_new, total_new, acc_new = new

    @pl.loop(0, count // 128 * heads)
    def _(step):
        head = step % heads
        at = pl.ds(pl.multiple_of(step // heads * 128, 128), 128)
        low = head * head_dim
        start = low // 128 * 128
        columns = pl.ds(pl.multiple_of(jnp.minimum(start, width - 256), 128), 256)
        skip = low - jnp.minimum(start, width - 256)
        from_row = low // 16 * 16
        window = pl.ds(pl.multiple_of(from_row, 16), 80)
        rows = pl.ds(pl.multiple_of(low, 8), head_dim)
        mine = lax.broadcasted_iota(jnp.int32, (heads, 128), 0) == head
        query = q_ref[at, columns]
        lane = lax.broadcasted_iota(jnp.int32, query.shape, 1)
        query = jnp.where((lane >= skip) & (lane < skip + head_dim), query, jnp.zeros((), BF16))
        scores = lax.dot_general(k_ref[:, columns], query, NT, preferred_element_type=F32)
        top = jnp.max(scores, axis=0, keepdims=True)
        if old is not None:
            top_old = jnp.sum(jnp.where(mine, old[0][:, at], 0.0), axis=0, keepdims=True)
            top = jnp.maximum(top, top_old)
            keep = jnp.exp2(top_old - top)
        weights = jnp.exp2(scores - top)
        total = jnp.sum(weights, axis=0, keepdims=True)
        mixed = jnp.dot(vt_ref[window, :], weights.astype(BF16), preferred_element_type=F32)
        mixed = jnp.where(low == from_row, mixed[:head_dim], mixed[80 - head_dim :])
        if old is not None:
            total_old = jnp.sum(jnp.where(mine, old[1][:, at], 0.0), axis=0, keepdims=True)
            total = total + total_old * keep
            mixed = mixed + old[2][rows, at] * keep
        top_new[:, at] = jnp.where(mine, top, top_new[:, at])
        total_new[:, at] = jnp.where(mine, total, total_new[:, at])
        acc_new[rows, at] = mixed


def keys_values(hidden, wk_ref, wvt_ref, k_ref, vt_ref):
    k_ref[...] = jnp.dot(hidden[...], wk_ref[...], preferred_element_type=F32).astype(BF16)
    vt_ref[...] = lax.dot_general(
        wvt_ref[...], hidden[...], NT, preferred_element_type=F32
    ).astype(BF16)


def norm_blocks(blocks, cond, column, hidden):
    width = hidden.shape[1]
    shift = cond[0:1, column : column + width]
    scale = cond[0:1, column + width : column + 2 * width]
    at = 0
    for block in blocks:
        rows = block.shape[0]
        hidden[at : at + rows, :] = modulated(block[...].astype(F32), shift, scale)
        at += rows


def condition(actions, table):
    vocab = table.shape[0]
    ids = lax.broadcasted_iota(jnp.int32, (8, vocab), 1)
    counts = jnp.zeros((8, vocab), F32)
    for i in range(actions.shape[1]):
        counts = counts + (ids == actions[0, i]).astype(F32)
    return jnp.dot(counts.astype(BF16), table, preferred_element_type=F32)


def first_kernel(heads, *refs):
    actions, table, own, mate, wq, wk, wv = refs[:7]
    cond, query, wk_v, wvt, top, total, acc = refs[7:14]
    ids, table_v, own_v, wq_v, wv_v, hidden, k_ref, vt_ref, sems = refs[14:]
    count, width = own_v.shape
    two = slice(2 * width, 4 * width)
    pairs = (
        (actions, ids),
        (table.at[:, 0 : 2 * width], table_v.at[:, 0 : 2 * width]),
        (own, own_v),
        (wq, wq_v),
        (wv, wv_v),
        (wk, wk_v),
        (table.at[:, two], table_v.at[:, two]),
    )
    copies = [pltpu.make_async_copy(src, dst, sems.at[i]) for i, (src, dst) in enumerate(pairs)]
    for copy in copies:
        copy.start()
    copies[0].wait()
    copies[1].wait()
    cond[:, 0 : 2 * width] = condition(ids, table_v[:, 0 : 2 * width])
    copies[2].wait()
    norm_blocks((own_v, mate), cond, 0, hidden)
    copies[3].wait()
    scale = math.log2(math.e) / math.sqrt(width // heads)
    query[...] = (
        jnp.dot(hidden[0:count, :], wq_v[...], preferred_element_type=F32) * scale
    ).astype(BF16)
    copies[4].wait()
    wvt[...] = wv_v[...].T
    copies[5].wait()
    keys_values(hidden, wk_v, wvt, k_ref, vt_ref)
    copies[6].wait()
    cond[:, two] = condition(ids, table_v[:, two])
    attend(query, k_ref, vt_ref, None, (top, total, acc), heads)


def more_kernel(heads, blocks, *refs):
    xs, refs = refs[:blocks], refs[blocks:]
    cond, query, wk, wvt, top, total, acc, top_new, total_new, acc_new = refs[:10]
    hidden, k_ref, vt_ref = refs[10:]
    norm_blocks(xs, cond, 0, hidden)
    keys_values(hidden, wk, wvt, k_ref, vt_ref)
    attend(query, k_ref, vt_ref, (top, total, acc), (top_new, total_new, acc_new), heads)


def last_kernel(heads, blocks, *refs):
    xs, refs = refs[:blocks], refs[blocks:]
    cond, query, wk, wvt, top, total, acc, own, w_out, first, hidden_two = refs[:11]
    top_new, total_new, acc_new, hidden, k_ref, vt_ref = refs[11:]
    width = own.shape[1]
    head_dim = width // heads
    norm_blocks(xs, cond, 0, hidden)
    keys_values(hidden, wk, wvt, k_ref, vt_ref)
    attend(query, k_ref, vt_ref, (top, total, acc), (top_new, total_new, acc_new), heads)
    pieces = [
        acc_new[h * head_dim : (h + 1) * head_dim, :] * (1.0 / total_new[h : h + 1, :])
        for h in range(heads)
    ]
    attended = jnp.concatenate(pieces, axis=0).astype(BF16).T
    y = own[...].astype(F32) + jnp.dot(attended, w_out[...], preferred_element_type=F32)
    rounded = y.astype(BF16)
    first[...] = rounded
    hidden_two[...] = modulated(
        rounded.astype(F32),
        cond[0:1, 2 * width : 3 * width],
        cond[0:1, 3 * width : 4 * width],
    )


def temporal_kernel(heads, *refs):
    history_start, x_ref, wq, wk, wv, out = refs[:6]
    hidden, q_ref, k_ref, vt_ref, ot = refs[6:]
    frames, tokens, width = x_ref.shape
    head_dim = width // heads
    groups = tokens // 8
    span = 8 * frames
    x = x_ref[...].astype(F32)
    for g in range(groups):
        hidden[g * span : (g + 1) * span, :] = (
            x[:, 8 * g : 8 * g + 8, :].reshape(span, width).astype(BF16)
        )
    vt_ref[...] = jnp.dot(hidden[...], wv[...], preferred_element_type=F32).astype(BF16).T
    scale = math.log2(math.e) / math.sqrt(head_dim)
    q_ref[...] = (jnp.dot(hidden[...], wq[...], preferred_element_type=F32) * scale).astype(BF16)
    k_ref[...] = jnp.dot(hidden[...], wk[...], preferred_element_type=F32).astype(BF16)
    cam_start = history_start[lax.axis_index("cam")]
    key = lax.broadcasted_iota(jnp.int32, (span, span), 0)
    ask = lax.broadcasted_iota(jnp.int32, (span, span), 1)
    same = (key % 8) == (ask % 8)
    frame_k, frame_q = key // 8, ask // 8
    allowed = same & ((frame_k == frame_q) | ((frame_k < frame_q) & (frame_k >= cam_start)))
    spans = [slice(g * span, (g + 1) * span) for g in range(groups)]

    def scores_of(pair):
        out = []
        for rows in spans:
            stacked, start = stacked_queries(q_ref[rows, :], pair, head_dim)
            both = lax.dot_general(
                k_ref[rows, start : start + 256], stacked, NT, preferred_element_type=F32
            )
            out.append((both[:, :span], both[:, span:]))
        return out

    ahead = scores_of(0)
    for pair in range(heads // 2):
        current = ahead
        if pair + 1 < heads // 2:
            ahead = scores_of(pair + 1)
        work = [
            (2 * pair + i, g, jnp.where(allowed, current[g][i], -1e30))
            for i in range(2)
            for g in range(groups)
        ]
        tops = [jnp.max(scores, axis=0, keepdims=True) for _, _, scores in work]
        weights = [jnp.exp2(item[2] - top) for item, top in zip(work, tops)]
        totals = [jnp.sum(w, axis=0, keepdims=True) for w in weights]
        for (head, g, _), w, total in zip(work, weights, totals):
            rows, window, inside = head_rows(head, head_dim)
            mixed = jnp.dot(
                vt_ref[window, spans[g]], w.astype(BF16), preferred_element_type=F32
            )[inside]
            ot[rows, spans[g]] = mixed * (1.0 / total)
    mixed = ot[...].astype(BF16).T.astype(F32)
    pieces = [mixed[g * span : (g + 1) * span, :].reshape(frames, 8, width) for g in range(groups)]
    out[...] = jnp.concatenate(pieces, axis=1).astype(BF16)


def output_kernel(first, mixed, t_out, out):
    rows, width = mixed.shape
    y = first[...].astype(F32) + jnp.dot(mixed[...], t_out[...], preferred_element_type=F32)
    out[...] = y.astype(BF16).reshape(out.shape)


def kernel_call(body, name, outs, scratch, operands, kinds, flops=0):
    space = {"s": pltpu.SMEM, "v": pltpu.VMEM, "h": pltpu.HBM}
    operands = [
        pltpu.with_memory_space_constraint(a, pltpu.HBM) if kind == "h" else a
        for a, kind in zip(operands, kinds)
    ]
    moved = sum(math.prod(a.shape) * a.dtype.itemsize for a in (*operands, *outs))
    return pl.pallas_call(
        body,
        name=name,
        out_shape=outs,
        in_specs=[pl.BlockSpec(memory_space=space[kind]) for kind in kinds],
        out_specs=[pl.BlockSpec(memory_space=pltpu.VMEM) for _ in outs],
        scratch_shapes=scratch,
        compiler_params=pltpu.CompilerParams(vmem_limit_bytes=VMEM_LIMIT),
        cost_estimate=pl.CostEstimate(flops=flops, bytes_accessed=moved, transcendentals=0),
    )(*operands)


def ring_routes():
    def index(y, core):
        return ((y // 2) * 2 + core) * 2 + y % 2

    places = [(y, core) for y in range(4) for core in range(2)]
    mate = [(index(y, core), index(y, 1 - core)) for y, core in places]
    partner = [(index(y, core), index(y ^ 1, core)) for y, core in places]
    other = [(index(y, core), index(3 - y, 1 - core)) for y, core in places]
    return mate, partner, other


def shards(
    latents,
    actions,
    history_start,
    mod_table,
    w_query,
    w_key,
    w_value,
    w_out,
    t_query,
    t_key,
    t_value,
    t_out,
):
    rows, width = latents.shape[2:]
    heads = HEADS
    frames = lax.axis_size("frame")
    own = latents[0, 0]
    mate, partner, other = ring_routes()
    half = rows // 2

    def sds(shape, dtype):
        return jax.ShapeDtypeStruct(shape, dtype)

    def buffer(*shape, dtype=BF16):
        return pltpu.VMEM(shape, dtype)

    def send(block, route):
        return lax.ppermute(block, RING, route)

    def projected(keys):
        return [buffer(keys, width), buffer(keys, width), buffer(width, keys)]

    def cost(keys):
        return 2 * unit * keys // rows + 4 * rows * keys * 256 * heads

    unit = 2 * rows * width * width
    weight = buffer(width, width)
    state = [sds((heads, rows), F32), sds((heads, rows), F32), sds((width, rows), F32)]
    low, high = own[:half], own[half:]
    other_low = send(low, other)
    partner_high = send(high, partner)
    from_mate = send(own, mate)
    low, high, from_mate = lax.optimization_barrier((low, high, from_mate))
    other_high = send(high, other)
    partner_low = send(low, partner)
    cond, query, wk, wvt, *held = kernel_call(
        functools.partial(first_kernel, heads),
        "cross_first",
        [sds((8, 4 * width), F32), sds((rows, width), BF16)]
        + [sds((width, width), BF16)] * 2
        + state,
        [pltpu.SMEM(actions.shape, jnp.int32)]
        + [buffer(*mod_table.shape), buffer(rows, width), weight, weight]
        + projected(2 * rows)
        + [pltpu.SemaphoreType.DMA((7,))],
        (actions, mod_table, own, from_mate, w_query, w_key, w_value),
        "hhhvhhh",
        flops=unit + cost(2 * rows),
    )
    other_low, partner_high, held = lax.optimization_barrier((other_low, partner_high, held))
    far_low = send(other_low, partner)
    far_high = send(partner_high, other)
    mate_high = send(partner_high, mate)
    partner_low, other_high, held = lax.optimization_barrier((partner_low, other_high, held))
    mate_low = send(partner_low, mate)
    held = kernel_call(
        functools.partial(more_kernel, heads, 4),
        "cross_second",
        state,
        projected(2 * rows),
        (other_low, partner_high, other_high, partner_low, cond, query, wk, wvt, *held),
        "v" * 11,
        flops=cost(2 * rows),
    )
    first, hidden_two = kernel_call(
        functools.partial(last_kernel, heads, 4),
        "cross_last",
        [sds((rows, width), BF16), sds((rows, width), BF16)],
        [pltpu.VMEM(s.shape, s.dtype) for s in state] + projected(2 * rows),
        (mate_high, mate_low, far_low, far_high, cond, query, wk, wvt, *held, own, w_out),
        "v" * 13,
        flops=cost(2 * rows) + unit,
    )
    share = rows // frames
    turned = lax.all_to_all(
        hidden_two.reshape(frames, share, width), "frame", 0, 0, tiled=True
    )
    (mixed,) = kernel_call(
        functools.partial(temporal_kernel, heads),
        "temporal",
        [sds((frames, share, width), BF16)],
        [buffer(rows, width)] * 3 + [buffer(width, rows), buffer(width, rows, dtype=F32)],
        (history_start, turned, t_query, t_key, t_value),
        "svvvv",
        flops=4 * unit,
    )
    back = lax.all_to_all(mixed, "frame", 0, 0, tiled=True).reshape(rows, width)
    (result,) = kernel_call(
        output_kernel,
        "output",
        [sds((1, 1, rows, width), BF16)],
        [],
        (first, back, t_out),
        "vvv",
        flops=unit,
    )
    return result


def solution(mesh):
    in_specs = (
        P("cam", "frame", "tok", None),
        P("frame", None),
        P(),
        P(),
        P(),
        P(),
        P(),
        P(),
        P(),
        P(),
        P(),
        P(),
    )
    out_specs = P("cam", "frame", "tok", None)
    return jax.shard_map(shards, mesh=mesh, in_specs=in_specs, out_specs=out_specs, check_vma=False)
```

```python
import functools
import math

import jax
import jax.numpy as jnp
from jax import lax
from jax.experimental import pallas as pl
from jax.experimental.pallas import tpu as pltpu
from jax.sharding import PartitionSpec as P

HEADS = 16
VMEM_LIMIT = 26 * 1024 * 1024
F32, BF16 = jnp.float32, jnp.bfloat16
NT = (((1,), (1,)), ((), ()))
TN = (((0,), (0,)), ((), ()))
RING = ("cam", "tok")


def modulated(values, shift, scale):
    mean = jnp.mean(values, axis=-1, keepdims=True)
    centred = values - mean
    spread = jnp.mean(centred * centred, axis=-1, keepdims=True)
    return (centred * lax.rsqrt(spread + 1e-06) * (1.0 + scale) + shift).astype(BF16)


def stacked_queries(query, pair, head_dim):
    start = 2 * pair * head_dim // 128 * 128
    window = query[:, start : start + 256]
    lane = lax.broadcasted_iota(jnp.int32, window.shape, 1) + start
    low = 2 * pair * head_dim
    zero = jnp.zeros((), query.dtype)
    parts = [
        jnp.where((lane >= low + i * head_dim) & (lane < low + (i + 1) * head_dim), window, zero)
        for i in range(2)
    ]
    return jnp.concatenate(parts, axis=0), start


def head_rows(head, head_dim):
    low = head * head_dim
    start = low // 16 * 16
    return slice(low, low + head_dim), slice(start, start + 80), slice(low - start, low - start + head_dim)


def attend(q_ref, k_ref, vt_ref, old, new, heads):
    count, width = q_ref.shape
    head_dim = width // heads
    top_new, total_new, acc_new = new

    def scores_of(pair):
        stacked, start = stacked_queries(q_ref[...], pair, head_dim)
        scores = lax.dot_general(
            k_ref[:, start : start + 256], stacked, NT, preferred_element_type=F32
        )
        return scores[:, :count], scores[:, count:]

    if old is None:
        own_key = q_ref[...] * k_ref[0:count, :]
        owner = lax.broadcasted_iota(jnp.int32, (heads, width), 1) // head_dim
        pick = (owner == lax.broadcasted_iota(jnp.int32, (heads, width), 0)).astype(BF16)
        top_new[...] = lax.dot_general(pick, own_key, NT, preferred_element_type=F32)
    else:
        top_new[...] = old[0][...]
    ahead = scores_of(0)
    for pair in range(heads // 2):
        current = ahead
        if pair + 1 < heads // 2:
            ahead = scores_of(pair + 1)
        for i in range(2):
            head = 2 * pair + i
            scores = current[i]
            rows, window, inside = head_rows(head, head_dim)
            top = top_new[head : head + 1, :]
            weights = jnp.exp2(scores - top)
            total = jnp.sum(weights, axis=0, keepdims=True)
            mixed = jnp.dot(
                vt_ref[window, :], weights.astype(BF16), preferred_element_type=F32
            )[inside]
            if old is not None:
                total = total + old[1][head : head + 1, :]
                mixed = mixed + old[2][rows, :]
            total_new[head : head + 1, :] = total
            acc_new[rows, :] = mixed

    sums = total_new[...]
    safe = (jnp.max(sums) < 2.0**60) & (jnp.min(sums) > 2.0**-60)

    @pl.when(jnp.logical_not(safe))
    def _():
        attend_with_maximum(q_ref, k_ref, vt_ref, old, new, heads)


def attend_with_maximum(q_ref, k_ref, vt_ref, old, new, heads):
    count, width = q_ref.shape
    head_dim = width // heads
    top_new, total_new, acc_new = new

    @pl.loop(0, count // 128 * heads)
    def _(step):
        head = step % heads
        at = pl.ds(pl.multiple_of(step // heads * 128, 128), 128)
        low = head * head_dim
        start = low // 128 * 128
        columns = pl.ds(pl.multiple_of(jnp.minimum(start, width - 256), 128), 256)
        skip = low - jnp.minimum(start, width - 256)
        from_row = low // 16 * 16
        window = pl.ds(pl.multiple_of(from_row, 16), 80)
        rows = pl.ds(pl.multiple_of(low, 8), head_dim)
        mine = lax.broadcasted_iota(jnp.int32, (heads, 128), 0) == head
        query = q_ref[at, columns]
        lane = lax.broadcasted_iota(jnp.int32, query.shape, 1)
        query = jnp.where((lane >= skip) & (lane < skip + head_dim), query, jnp.zeros((), BF16))
        scores = lax.dot_general(k_ref[:, columns], query, NT, preferred_element_type=F32)
        top = jnp.max(scores, axis=0, keepdims=True)
        if old is not None:
            top_old = jnp.sum(jnp.where(mine, old[0][:, at], 0.0), axis=0, keepdims=True)
            top = jnp.maximum(top, top_old)
            keep = jnp.exp2(top_old - top)
        weights = jnp.exp2(scores - top)
        total = jnp.sum(weights, axis=0, keepdims=True)
        mixed = jnp.dot(vt_ref[window, :], weights.astype(BF16), preferred_element_type=F32)
        mixed = jnp.where(low == from_row, mixed[:head_dim], mixed[80 - head_dim :])
        if old is not None:
            total_old = jnp.sum(jnp.where(mine, old[1][:, at], 0.0), axis=0, keepdims=True)
            total = total + total_old * keep
            mixed = mixed + old[2][rows, at] * keep
        top_new[:, at] = jnp.where(mine, top, top_new[:, at])
        total_new[:, at] = jnp.where(mine, total, total_new[:, at])
        acc_new[rows, at] = mixed


def keys_values(hidden, wk_ref, wvt_ref, k_ref, vt_ref):
    k_ref[...] = jnp.dot(hidden[...], wk_ref[...], preferred_element_type=F32).astype(BF16)
    vt_ref[...] = lax.dot_general(
        wvt_ref[...], hidden[...], NT, preferred_element_type=F32
    ).astype(BF16)


def norm_blocks(blocks, cond, column, hidden):
    width = hidden.shape[1]
    shift = cond[0:1, column : column + width]
    scale = cond[0:1, column + width : column + 2 * width]
    at = 0
    for block in blocks:
        rows = block.shape[0]
        hidden[at : at + rows, :] = modulated(block[...].astype(F32), shift, scale)
        at += rows


def condition(actions, table):
    vocab = table.shape[0]
    ids = lax.broadcasted_iota(jnp.int32, (8, vocab), 1)
    counts = jnp.zeros((8, vocab), F32)
    for i in range(actions.shape[1]):
        counts = counts + (ids == actions[0, i]).astype(F32)
    return jnp.dot(counts.astype(BF16), table, preferred_element_type=F32)


def first_kernel(heads, *refs):
    actions, table, own, mate, wq, wk, wv = refs[:7]
    cond, query, wk_v, wvt, top, total, acc = refs[7:14]
    ids, table_v, own_v, wq_v, wv_v, hidden, k_ref, vt_ref, sems = refs[14:]
    count, width = own_v.shape
    two = slice(2 * width, 4 * width)
    pairs = (
        (actions, ids),
        (table.at[:, 0 : 2 * width], table_v.at[:, 0 : 2 * width]),
        (own, own_v),
        (wq, wq_v),
        (wv, wv_v),
        (wk, wk_v),
        (table.at[:, two], table_v.at[:, two]),
    )
    copies = [pltpu.make_async_copy(src, dst, sems.at[i]) for i, (src, dst) in enumerate(pairs)]
    for copy in copies:
        copy.start()
    copies[0].wait()
    copies[1].wait()
    cond[:, 0 : 2 * width] = condition(ids, table_v[:, 0 : 2 * width])
    copies[2].wait()
    norm_blocks((own_v, mate), cond, 0, hidden)
    copies[3].wait()
    scale = math.log2(math.e) / math.sqrt(width // heads)
    query[...] = (
        jnp.dot(hidden[0:count, :], wq_v[...], preferred_element_type=F32) * scale
    ).astype(BF16)
    copies[4].wait()
    wvt[...] = wv_v[...].T
    copies[5].wait()
    keys_values(hidden, wk_v, wvt, k_ref, vt_ref)
    copies[6].wait()
    cond[:, two] = condition(ids, table_v[:, two])
    attend(query, k_ref, vt_ref, None, (top, total, acc), heads)


def more_kernel(heads, blocks, *refs):
    xs, refs = refs[:blocks], refs[blocks:]
    cond, query, wk, wvt, top, total, acc, top_new, total_new, acc_new = refs[:10]
    hidden, k_ref, vt_ref = refs[10:]
    norm_blocks(xs, cond, 0, hidden)
    keys_values(hidden, wk, wvt, k_ref, vt_ref)
    attend(query, k_ref, vt_ref, (top, total, acc), (top_new, total_new, acc_new), heads)


def last_kernel(heads, blocks, *refs):
    xs, refs = refs[:blocks], refs[blocks:]
    cond, query, wk, wvt, top, total, acc, own, w_out, first, hidden_two = refs[:11]
    top_new, total_new, acc_new, hidden, k_ref, vt_ref = refs[11:]
    width = own.shape[1]
    head_dim = width // heads
    norm_blocks(xs, cond, 0, hidden)
    keys_values(hidden, wk, wvt, k_ref, vt_ref)
    attend(query, k_ref, vt_ref, (top, total, acc), (top_new, total_new, acc_new), heads)
    pieces = [
        acc_new[h * head_dim : (h + 1) * head_dim, :] * (1.0 / total_new[h : h + 1, :])
        for h in range(heads)
    ]
    attended = jnp.concatenate(pieces, axis=0).astype(BF16).T
    y = own[...].astype(F32) + jnp.dot(attended, w_out[...], preferred_element_type=F32)
    rounded = y.astype(BF16)
    first[...] = rounded
    hidden_two[...] = modulated(
        rounded.astype(F32),
        cond[0:1, 2 * width : 3 * width],
        cond[0:1, 3 * width : 4 * width],
    )


def temporal_kernel(heads, *refs):
    history_start, x_ref, wq, wk, wv, out = refs[:6]
    hidden, q_ref, k_ref, vt_ref, ot = refs[6:]
    frames, tokens, width = x_ref.shape
    head_dim = width // heads
    groups = tokens // 8
    span = 8 * frames
    x = x_ref[...].astype(F32)
    for g in range(groups):
        hidden[g * span : (g + 1) * span, :] = (
            x[:, 8 * g : 8 * g + 8, :].reshape(span, width).astype(BF16)
        )
    vt_ref[...] = jnp.dot(hidden[...], wv[...], preferred_element_type=F32).astype(BF16).T
    scale = math.log2(math.e) / math.sqrt(head_dim)
    q_ref[...] = (jnp.dot(hidden[...], wq[...], preferred_element_type=F32) * scale).astype(BF16)
    k_ref[...] = jnp.dot(hidden[...], wk[...], preferred_element_type=F32).astype(BF16)
    cam_start = history_start[lax.axis_index("cam")]
    key = lax.broadcasted_iota(jnp.int32, (span, span), 0)
    ask = lax.broadcasted_iota(jnp.int32, (span, span), 1)
    same = (key % 8) == (ask % 8)
    frame_k, frame_q = key // 8, ask // 8
    allowed = same & ((frame_k == frame_q) | ((frame_k < frame_q) & (frame_k >= cam_start)))
    spans = [slice(g * span, (g + 1) * span) for g in range(groups)]

    def scores_of(pair):
        out = []
        for rows in spans:
            stacked, start = stacked_queries(q_ref[rows, :], pair, head_dim)
            both = lax.dot_general(
                k_ref[rows, start : start + 256], stacked, NT, preferred_element_type=F32
            )
            out.append((both[:, :span], both[:, span:]))
        return out

    ahead = scores_of(0)
    for pair in range(heads // 2):
        current = ahead
        if pair + 1 < heads // 2:
            ahead = scores_of(pair + 1)
        work = [
            (2 * pair + i, g, jnp.where(allowed, current[g][i], -1e30))
            for i in range(2)
            for g in range(groups)
        ]
        tops = [jnp.max(scores, axis=0, keepdims=True) for _, _, scores in work]
        weights = [jnp.exp2(item[2] - top) for item, top in zip(work, tops)]
        totals = [jnp.sum(w, axis=0, keepdims=True) for w in weights]
        for (head, g, _), w, total in zip(work, weights, totals):
            rows, window, inside = head_rows(head, head_dim)
            mixed = jnp.dot(
                vt_ref[window, spans[g]], w.astype(BF16), preferred_element_type=F32
            )[inside]
            ot[rows, spans[g]] = mixed * (1.0 / total)
    mixed = ot[...].astype(BF16).T.astype(F32)
    pieces = [mixed[g * span : (g + 1) * span, :].reshape(frames, 8, width) for g in range(groups)]
    out[...] = jnp.concatenate(pieces, axis=1).astype(BF16)


def output_kernel(first, mixed, t_out, out, done, sems):
    rows = mixed.shape[0]
    step = 128
    copies = []
    for i, at in enumerate(range(0, rows, step)):
        part = slice(at, at + step)
        y = first[part, :].astype(F32) + jnp.dot(
            mixed[part, :], t_out[...], preferred_element_type=F32
        )
        done[part, :] = y.astype(BF16)
        copies.append(
            pltpu.make_async_copy(done.at[part, :], out.at[0, 0, part, :], sems.at[i])
        )
        copies[-1].start()
    for copy in copies:
        copy.wait()


def kernel_call(body, name, outs, scratch, operands, kinds, flops=0, out_space=pltpu.VMEM):
    space = {"s": pltpu.SMEM, "v": pltpu.VMEM, "h": pltpu.HBM}
    operands = [
        pltpu.with_memory_space_constraint(a, pltpu.HBM) if kind == "h" else a
        for a, kind in zip(operands, kinds)
    ]
    moved = sum(math.prod(a.shape) * a.dtype.itemsize for a in (*operands, *outs))
    return pl.pallas_call(
        body,
        name=name,
        out_shape=outs,
        in_specs=[pl.BlockSpec(memory_space=space[kind]) for kind in kinds],
        out_specs=[pl.BlockSpec(memory_space=out_space) for _ in outs],
        scratch_shapes=scratch,
        compiler_params=pltpu.CompilerParams(vmem_limit_bytes=VMEM_LIMIT),
        cost_estimate=pl.CostEstimate(flops=flops, bytes_accessed=moved, transcendentals=0),
    )(*operands)


def ring_routes():
    def index(y, core):
        return ((y // 2) * 2 + core) * 2 + y % 2

    places = [(y, core) for y in range(4) for core in range(2)]
    mate = [(index(y, core), index(y, 1 - core)) for y, core in places]
    partner = [(index(y, core), index(y ^ 1, core)) for y, core in places]
    other = [(index(y, core), index(3 - y, 1 - core)) for y, core in places]
    return mate, partner, other


def shards(
    latents,
    actions,
    history_start,
    mod_table,
    w_query,
    w_key,
    w_value,
    w_out,
    t_query,
    t_key,
    t_value,
    t_out,
):
    rows, width = latents.shape[2:]
    heads = HEADS
    frames = lax.axis_size("frame")
    own = latents[0, 0]
    mate, partner, other = ring_routes()
    half = rows // 2

    def sds(shape, dtype):
        return jax.ShapeDtypeStruct(shape, dtype)

    def buffer(*shape, dtype=BF16):
        return pltpu.VMEM(shape, dtype)

    def send(block, route):
        return lax.ppermute(block, RING, route)

    def projected(keys):
        return [buffer(keys, width), buffer(keys, width), buffer(width, keys)]

    def cost(keys):
        return 2 * unit * keys // rows + 4 * rows * keys * 256 * heads

    unit = 2 * rows * width * width
    weight = buffer(width, width)
    state = [sds((heads, rows), F32), sds((heads, rows), F32), sds((width, rows), F32)]
    low, high = own[:half], own[half:]
    other_low = send(low, other)
    partner_high = send(high, partner)
    from_mate = send(own, mate)
    low, high, from_mate = lax.optimization_barrier((low, high, from_mate))
    other_high = send(high, other)
    partner_low = send(low, partner)
    cond, query, wk, wvt, *held = kernel_call(
        functools.partial(first_kernel, heads),
        "cross_first",
        [sds((8, 4 * width), F32), sds((rows, width), BF16)]
        + [sds((width, width), BF16)] * 2
        + state,
        [pltpu.SMEM(actions.shape, jnp.int32)]
        + [buffer(*mod_table.shape), buffer(rows, width), weight, weight]
        + projected(2 * rows)
        + [pltpu.SemaphoreType.DMA((7,))],
        (actions, mod_table, own, from_mate, w_query, w_key, w_value),
        "hhhvhhh",
        flops=unit + cost(2 * rows),
    )
    other_low, partner_high, held = lax.optimization_barrier((other_low, partner_high, held))
    far_low = send(other_low, partner)
    far_high = send(partner_high, other)
    mate_high = send(partner_high, mate)
    partner_low, other_high, held = lax.optimization_barrier((partner_low, other_high, held))
    mate_low = send(partner_low, mate)
    held = kernel_call(
        functools.partial(more_kernel, heads, 4),
        "cross_second",
        state,
        projected(2 * rows),
        (other_low, partner_high, other_high, partner_low, cond, query, wk, wvt, *held),
        "v" * 11,
        flops=cost(2 * rows),
    )
    first, hidden_two = kernel_call(
        functools.partial(last_kernel, heads, 4),
        "cross_last",
        [sds((rows, width), BF16), sds((rows, width), BF16)],
        [pltpu.VMEM(s.shape, s.dtype) for s in state] + projected(2 * rows),
        (mate_high, mate_low, far_low, far_high, cond, query, wk, wvt, *held, own, w_out),
        "v" * 13,
        flops=cost(2 * rows) + unit,
    )
    share = rows // frames
    turned = lax.all_to_all(
        hidden_two.reshape(frames, share, width), "frame", 0, 0, tiled=True
    )
    (mixed,) = kernel_call(
        functools.partial(temporal_kernel, heads),
        "temporal",
        [sds((frames, share, width), BF16)],
        [buffer(rows, width)] * 3 + [buffer(width, rows), buffer(width, rows, dtype=F32)],
        (history_start, turned, t_query, t_key, t_value),
        "svvvv",
        flops=4 * unit,
    )
    back = lax.all_to_all(mixed, "frame", 0, 0, tiled=True).reshape(rows, width)
    (result,) = kernel_call(
        output_kernel,
        "output",
        [sds((1, 1, rows, width), BF16)],
        [buffer(rows, width), pltpu.SemaphoreType.DMA((rows // 128,))],
        (first, back, t_out),
        "vvv",
        flops=unit,
        out_space=pl.ANY,
    )
    return result


def solution(mesh):
    in_specs = (
        P("cam", "frame", "tok", None),
        P("frame", None),
        P(),
        P(),
        P(),
        P(),
        P(),
        P(),
        P(),
        P(),
        P(),
        P(),
    )
    out_specs = P("cam", "frame", "tok", None)
    return jax.shard_map(shards, mesh=mesh, in_specs=in_specs, out_specs=out_specs, check_vma=False)
```

```python
import functools
import math

import jax
import jax.numpy as jnp
from jax import lax
from jax.experimental import pallas as pl
from jax.experimental.pallas import tpu as pltpu
from jax.sharding import PartitionSpec as P

HEADS = 16
VMEM_LIMIT = 26 * 1024 * 1024
F32, BF16 = jnp.float32, jnp.bfloat16
NT = (((1,), (1,)), ((), ()))
TN = (((0,), (0,)), ((), ()))
RING = ("cam", "tok")


def modulated(values, shift, scale):
    mean = jnp.mean(values, axis=-1, keepdims=True)
    centred = values - mean
    spread = jnp.mean(centred * centred, axis=-1, keepdims=True)
    return (centred * lax.rsqrt(spread + 1e-06) * (1.0 + scale) + shift).astype(BF16)


def stacked_queries(query, pair, head_dim):
    start = 2 * pair * head_dim // 128 * 128
    window = query[:, start : start + 256]
    lane = lax.broadcasted_iota(jnp.int32, window.shape, 1) + start
    low = 2 * pair * head_dim
    zero = jnp.zeros((), query.dtype)
    parts = [
        jnp.where((lane >= low + i * head_dim) & (lane < low + (i + 1) * head_dim), window, zero)
        for i in range(2)
    ]
    return jnp.concatenate(parts, axis=0), start


def head_rows(head, head_dim):
    low = head * head_dim
    start = low // 16 * 16
    return slice(low, low + head_dim), slice(start, start + 80), slice(low - start, low - start + head_dim)


def attend(q_ref, k_ref, vt_ref, old, new, heads):
    count, width = q_ref.shape
    head_dim = width // heads
    top_new, total_new, acc_new = new

    def scores_of(pair):
        stacked, start = stacked_queries(q_ref[...], pair, head_dim)
        scores = lax.dot_general(
            k_ref[:, start : start + 256], stacked, NT, preferred_element_type=F32
        )
        return scores[:, :count], scores[:, count:]

    if old is None:
        own_key = q_ref[...] * k_ref[0:count, :]
        owner = lax.broadcasted_iota(jnp.int32, (heads, width), 1) // head_dim
        pick = (owner == lax.broadcasted_iota(jnp.int32, (heads, width), 0)).astype(BF16)
        top_new[...] = lax.dot_general(pick, own_key, NT, preferred_element_type=F32)
    else:
        top_new[...] = old[0][...]
    ahead = scores_of(0)
    for pair in range(heads // 2):
        current = ahead
        if pair + 1 < heads // 2:
            ahead = scores_of(pair + 1)
        for i in range(2):
            head = 2 * pair + i
            scores = current[i]
            rows, window, inside = head_rows(head, head_dim)
            top = top_new[head : head + 1, :]
            weights = jnp.exp2(scores - top)
            total = jnp.sum(weights, axis=0, keepdims=True)
            mixed = jnp.dot(
                vt_ref[window, :], weights.astype(BF16), preferred_element_type=F32
            )[inside]
            if old is not None:
                total = total + old[1][head : head + 1, :]
                mixed = mixed + old[2][rows, :]
            total_new[head : head + 1, :] = total
            acc_new[rows, :] = mixed

    sums = total_new[...]
    safe = (jnp.max(sums) < 2.0**60) & (jnp.min(sums) > 2.0**-60)

    @pl.when(jnp.logical_not(safe))
    def _():
        attend_with_maximum(q_ref, k_ref, vt_ref, old, new, heads)


def attend_with_maximum(q_ref, k_ref, vt_ref, old, new, heads):
    count, width = q_ref.shape
    head_dim = width // heads
    top_new, total_new, acc_new = new

    @pl.loop(0, count // 128 * heads)
    def _(step):
        head = step % heads
        at = pl.ds(pl.multiple_of(step // heads * 128, 128), 128)
        low = head * head_dim
        start = low // 128 * 128
        columns = pl.ds(pl.multiple_of(jnp.minimum(start, width - 256), 128), 256)
        skip = low - jnp.minimum(start, width - 256)
        from_row = low // 16 * 16
        window = pl.ds(pl.multiple_of(from_row, 16), 80)
        rows = pl.ds(pl.multiple_of(low, 8), head_dim)
        mine = lax.broadcasted_iota(jnp.int32, (heads, 128), 0) == head
        query = q_ref[at, columns]
        lane = lax.broadcasted_iota(jnp.int32, query.shape, 1)
        query = jnp.where((lane >= skip) & (lane < skip + head_dim), query, jnp.zeros((), BF16))
        scores = lax.dot_general(k_ref[:, columns], query, NT, preferred_element_type=F32)
        top = jnp.max(scores, axis=0, keepdims=True)
        if old is not None:
            top_old = jnp.sum(jnp.where(mine, old[0][:, at], 0.0), axis=0, keepdims=True)
            top = jnp.maximum(top, top_old)
            keep = jnp.exp2(top_old - top)
        weights = jnp.exp2(scores - top)
        total = jnp.sum(weights, axis=0, keepdims=True)
        mixed = jnp.dot(vt_ref[window, :], weights.astype(BF16), preferred_element_type=F32)
        mixed = jnp.where(low == from_row, mixed[:head_dim], mixed[80 - head_dim :])
        if old is not None:
            total_old = jnp.sum(jnp.where(mine, old[1][:, at], 0.0), axis=0, keepdims=True)
            total = total + total_old * keep
            mixed = mixed + old[2][rows, at] * keep
        top_new[:, at] = jnp.where(mine, top, top_new[:, at])
        total_new[:, at] = jnp.where(mine, total, total_new[:, at])
        acc_new[rows, at] = mixed


def keys_values(hidden, wk_ref, wvt_ref, k_ref, vt_ref):
    k_ref[...] = jnp.dot(hidden[...], wk_ref[...], preferred_element_type=F32).astype(BF16)
    vt_ref[...] = lax.dot_general(
        wvt_ref[...], hidden[...], NT, preferred_element_type=F32
    ).astype(BF16)


def norm_blocks(blocks, cond, column, hidden):
    width = hidden.shape[1]
    shift = cond[0:1, column : column + width]
    scale = cond[0:1, column + width : column + 2 * width]
    at = 0
    for block in blocks:
        rows = block.shape[0]
        hidden[at : at + rows, :] = modulated(block[...].astype(F32), shift, scale)
        at += rows


def condition(actions, table):
    vocab = table.shape[0]
    ids = lax.broadcasted_iota(jnp.int32, (8, vocab), 1)
    counts = jnp.zeros((8, vocab), F32)
    for i in range(actions.shape[1]):
        counts = counts + (ids == actions[0, i]).astype(F32)
    return jnp.dot(counts.astype(BF16), table, preferred_element_type=F32)


def first_kernel(heads, *refs):
    actions, table, own, mate, wq, wk, wv = refs[:7]
    cond, query, wk_v, wvt, top, total, acc = refs[7:14]
    ids, table_v, own_v, wq_v, wv_v, hidden, k_ref, vt_ref, sems = refs[14:]
    count, width = own_v.shape
    two = slice(2 * width, 4 * width)
    pairs = (
        (actions, ids),
        (own, own_v),
        (table.at[:, 0 : 2 * width], table_v.at[:, 0 : 2 * width]),
        (wq, wq_v),
        (wv, wv_v),
        (wk, wk_v),
        (table.at[:, two], table_v.at[:, two]),
    )
    copies = [pltpu.make_async_copy(src, dst, sems.at[i]) for i, (src, dst) in enumerate(pairs)]
    for copy in copies:
        copy.start()
    copies[0].wait()
    copies[2].wait()
    cond[:, 0 : 2 * width] = condition(ids, table_v[:, 0 : 2 * width])
    copies[1].wait()
    norm_blocks((own_v, mate), cond, 0, hidden)
    copies[3].wait()
    scale = math.log2(math.e) / math.sqrt(width // heads)
    query[...] = (
        jnp.dot(hidden[0:count, :], wq_v[...], preferred_element_type=F32) * scale
    ).astype(BF16)
    copies[4].wait()
    wvt[...] = wv_v[...].T
    copies[5].wait()
    keys_values(hidden, wk_v, wvt, k_ref, vt_ref)
    copies[6].wait()
    cond[:, two] = condition(ids, table_v[:, two])
    attend(query, k_ref, vt_ref, None, (top, total, acc), heads)


def more_kernel(heads, blocks, *refs):
    xs, refs = refs[:blocks], refs[blocks:]
    cond, query, wk, wvt, top, total, acc, top_new, total_new, acc_new = refs[:10]
    hidden, k_ref, vt_ref = refs[10:]
    norm_blocks(xs, cond, 0, hidden)
    keys_values(hidden, wk, wvt, k_ref, vt_ref)
    attend(query, k_ref, vt_ref, (top, total, acc), (top_new, total_new, acc_new), heads)


def last_kernel(heads, blocks, *refs):
    xs, refs = refs[:blocks], refs[blocks:]
    cond, query, wk, wvt, top, total, acc, own, w_out, first, hidden_two = refs[:11]
    top_new, total_new, acc_new, hidden, k_ref, vt_ref = refs[11:]
    width = own.shape[1]
    head_dim = width // heads
    norm_blocks(xs, cond, 0, hidden)
    keys_values(hidden, wk, wvt, k_ref, vt_ref)
    attend(query, k_ref, vt_ref, (top, total, acc), (top_new, total_new, acc_new), heads)
    pieces = [
        acc_new[h * head_dim : (h + 1) * head_dim, :] * (1.0 / total_new[h : h + 1, :])
        for h in range(heads)
    ]
    attended = jnp.concatenate(pieces, axis=0).astype(BF16).T
    y = own[...].astype(F32) + jnp.dot(attended, w_out[...], preferred_element_type=F32)
    rounded = y.astype(BF16)
    first[...] = rounded
    hidden_two[...] = modulated(
        rounded.astype(F32),
        cond[0:1, 2 * width : 3 * width],
        cond[0:1, 3 * width : 4 * width],
    )


def temporal_kernel(heads, *refs):
    history_start, x_ref, wq, wk, wv, out = refs[:6]
    hidden, q_ref, k_ref, vt_ref, ot = refs[6:]
    frames, tokens, width = x_ref.shape
    head_dim = width // heads
    groups = tokens // 8
    span = 8 * frames
    x = x_ref[...].astype(F32)
    for g in range(groups):
        hidden[g * span : (g + 1) * span, :] = (
            x[:, 8 * g : 8 * g + 8, :].reshape(span, width).astype(BF16)
        )
    vt_ref[...] = jnp.dot(hidden[...], wv[...], preferred_element_type=F32).astype(BF16).T
    scale = math.log2(math.e) / math.sqrt(head_dim)
    q_ref[...] = (jnp.dot(hidden[...], wq[...], preferred_element_type=F32) * scale).astype(BF16)
    k_ref[...] = jnp.dot(hidden[...], wk[...], preferred_element_type=F32).astype(BF16)
    cam_start = history_start[lax.axis_index("cam")]
    key = lax.broadcasted_iota(jnp.int32, (span, span), 0)
    ask = lax.broadcasted_iota(jnp.int32, (span, span), 1)
    same = (key % 8) == (ask % 8)
    frame_k, frame_q = key // 8, ask // 8
    allowed = same & ((frame_k == frame_q) | ((frame_k < frame_q) & (frame_k >= cam_start)))
    spans = [slice(g * span, (g + 1) * span) for g in range(groups)]

    def scores_of(pair):
        out = []
        for rows in spans:
            stacked, start = stacked_queries(q_ref[rows, :], pair, head_dim)
            both = lax.dot_general(
                k_ref[rows, start : start + 256], stacked, NT, preferred_element_type=F32
            )
            out.append((both[:, :span], both[:, span:]))
        return out

    ahead = scores_of(0)
    for pair in range(heads // 2):
        current = ahead
        if pair + 1 < heads // 2:
            ahead = scores_of(pair + 1)
        work = [
            (2 * pair + i, g, jnp.where(allowed, current[g][i], -1e30))
            for i in range(2)
            for g in range(groups)
        ]
        tops = [jnp.max(scores, axis=0, keepdims=True) for _, _, scores in work]
        weights = [jnp.exp2(item[2] - top) for item, top in zip(work, tops)]
        totals = [jnp.sum(w, axis=0, keepdims=True) for w in weights]
        for (head, g, _), w, total in zip(work, weights, totals):
            rows, window, inside = head_rows(head, head_dim)
            mixed = jnp.dot(
                vt_ref[window, spans[g]], w.astype(BF16), preferred_element_type=F32
            )[inside]
            ot[rows, spans[g]] = mixed * (1.0 / total)
    mixed = ot[...].astype(BF16).T.astype(F32)
    pieces = [mixed[g * span : (g + 1) * span, :].reshape(frames, 8, width) for g in range(groups)]
    out[...] = jnp.concatenate(pieces, axis=1).astype(BF16)


def output_kernel(first, mixed, t_out, out, done, sems):
    rows = mixed.shape[0]
    step = 128
    copies = []
    for i, at in enumerate(range(0, rows, step)):
        part = slice(at, at + step)
        y = first[part, :].astype(F32) + jnp.dot(
            mixed[part, :], t_out[...], preferred_element_type=F32
        )
        done[part, :] = y.astype(BF16)
        copies.append(
            pltpu.make_async_copy(done.at[part, :], out.at[0, 0, part, :], sems.at[i])
        )
        copies[-1].start()
    for copy in copies:
        copy.wait()


def kernel_call(body, name, outs, scratch, operands, kinds, flops=0, out_space=pltpu.VMEM):
    space = {"s": pltpu.SMEM, "v": pltpu.VMEM, "h": pltpu.HBM}
    operands = [
        pltpu.with_memory_space_constraint(a, pltpu.HBM) if kind == "h" else a
        for a, kind in zip(operands, kinds)
    ]
    moved = sum(math.prod(a.shape) * a.dtype.itemsize for a in (*operands, *outs))
    return pl.pallas_call(
        body,
        name=name,
        out_shape=outs,
        in_specs=[pl.BlockSpec(memory_space=space[kind]) for kind in kinds],
        out_specs=[pl.BlockSpec(memory_space=out_space) for _ in outs],
        scratch_shapes=scratch,
        compiler_params=pltpu.CompilerParams(vmem_limit_bytes=VMEM_LIMIT),
        cost_estimate=pl.CostEstimate(flops=flops, bytes_accessed=moved, transcendentals=0),
    )(*operands)


def ring_routes():
    def index(y, core):
        return ((y // 2) * 2 + core) * 2 + y % 2

    places = [(y, core) for y in range(4) for core in range(2)]
    mate = [(index(y, core), index(y, 1 - core)) for y, core in places]
    partner = [(index(y, core), index(y ^ 1, core)) for y, core in places]
    other = [(index(y, core), index(3 - y, 1 - core)) for y, core in places]
    return mate, partner, other


def shards(
    latents,
    actions,
    history_start,
    mod_table,
    w_query,
    w_key,
    w_value,
    w_out,
    t_query,
    t_key,
    t_value,
    t_out,
):
    rows, width = latents.shape[2:]
    heads = HEADS
    frames = lax.axis_size("frame")
    own = latents[0, 0]
    mate, partner, other = ring_routes()
    half = rows // 2

    def sds(shape, dtype):
        return jax.ShapeDtypeStruct(shape, dtype)

    def buffer(*shape, dtype=BF16):
        return pltpu.VMEM(shape, dtype)

    def send(block, route):
        return lax.ppermute(block, RING, route)

    def projected(keys):
        return [buffer(keys, width), buffer(keys, width), buffer(width, keys)]

    def cost(keys):
        return 2 * unit * keys // rows + 4 * rows * keys * 256 * heads

    unit = 2 * rows * width * width
    weight = buffer(width, width)
    state = [sds((heads, rows), F32), sds((heads, rows), F32), sds((width, rows), F32)]
    low, high = own[:half], own[half:]
    other_low = send(low, other)
    partner_high = send(high, partner)
    from_mate = send(own, mate)
    low, high, from_mate = lax.optimization_barrier((low, high, from_mate))
    other_high = send(high, other)
    partner_low = send(low, partner)
    cond, query, wk, wvt, *held = kernel_call(
        functools.partial(first_kernel, heads),
        "cross_first",
        [sds((8, 4 * width), F32), sds((rows, width), BF16)]
        + [sds((width, width), BF16)] * 2
        + state,
        [pltpu.SMEM(actions.shape, jnp.int32)]
        + [buffer(*mod_table.shape), buffer(rows, width), weight, weight]
        + projected(2 * rows)
        + [pltpu.SemaphoreType.DMA((7,))],
        (actions, mod_table, own, from_mate, w_query, w_key, w_value),
        "hhhvhhh",
        flops=unit + cost(2 * rows),
    )
    other_low, partner_high, held = lax.optimization_barrier((other_low, partner_high, held))
    far_low = send(other_low, partner)
    far_high = send(partner_high, other)
    mate_high = send(partner_high, mate)
    partner_low, other_high, held = lax.optimization_barrier((partner_low, other_high, held))
    mate_low = send(partner_low, mate)
    held = kernel_call(
        functools.partial(more_kernel, heads, 4),
        "cross_second",
        state,
        projected(2 * rows),
        (other_low, partner_high, other_high, partner_low, cond, query, wk, wvt, *held),
        "v" * 11,
        flops=cost(2 * rows),
    )
    first, hidden_two = kernel_call(
        functools.partial(last_kernel, heads, 4),
        "cross_last",
        [sds((rows, width), BF16), sds((rows, width), BF16)],
        [pltpu.VMEM(s.shape, s.dtype) for s in state] + projected(2 * rows),
        (mate_high, mate_low, far_low, far_high, cond, query, wk, wvt, *held, own, w_out),
        "v" * 13,
        flops=cost(2 * rows) + unit,
    )
    share = rows // frames
    turned = lax.all_to_all(
        hidden_two.reshape(frames, share, width), "frame", 0, 0, tiled=True
    )
    (mixed,) = kernel_call(
        functools.partial(temporal_kernel, heads),
        "temporal",
        [sds((frames, share, width), BF16)],
        [buffer(rows, width)] * 3 + [buffer(width, rows), buffer(width, rows, dtype=F32)],
        (history_start, turned, t_query, t_key, t_value),
        "svvvv",
        flops=4 * unit,
    )
    back = lax.all_to_all(mixed, "frame", 0, 0, tiled=True).reshape(rows, width)
    (result,) = kernel_call(
        output_kernel,
        "output",
        [sds((1, 1, rows, width), BF16)],
        [buffer(rows, width), pltpu.SemaphoreType.DMA((rows // 128,))],
        (first, back, t_out),
        "vvv",
        flops=unit,
        out_space=pl.ANY,
    )
    return result


def solution(mesh):
    in_specs = (
        P("cam", "frame", "tok", None),
        P("frame", None),
        P(),
        P(),
        P(),
        P(),
        P(),
        P(),
        P(),
        P(),
        P(),
        P(),
    )
    out_specs = P("cam", "frame", "tok", None)
    return jax.shard_map(shards, mesh=mesh, in_specs=in_specs, out_specs=out_specs, check_vma=False)
```
